256 devices in a mesh: ens: 4 (over y), space: 64 (over z, x, core).
Axes of the slice: x: 4, y: 4, z: 8, core: 2. Of those that a mesh axis runs over, the one named last changes fastest.
Arguments:
- latents: bfloat16 [8, 16384, 1024], P('ens', 'space'), may hold values from -6 to 6
- edge_index: int32 [32768, 4], P('space'), may hold values from 0 to 767, as said below
- edge_weight: float32 [32768, 4], P('space'), may hold values from 0.1 to 1
- truth: float32 [100, 32768], P(None, 'space'), may hold values from -6 to 6
- w_hidden: bfloat16 [1024, 1024], replicated, may hold values from -0.1875 to 0.1875
- output_weight: bfloat16 [1024, 100], replicated, may hold values from -0.1875 to 0.1875
Outputs:
- grad_latents: float32 [8, 16384, 1024], P('ens', 'space')
- grad_hidden: float32 [1024, 1024], P('space')
- grad_out: float32 [1024, 100], P('space')
The draws below stay inside these ranges and needn't reach their ends.
Inputs may be any that keep to these rules, and one draw needn't show every extreme that they name: edge_index of a grid point holds 4 distinct values, indexing the nodes of the bands below, own and above; the first band never points below and the last never above.
All inputs are finite; a program needn't handle non-finite values.
Results may differ from the reference program's by a relative error of at most 0.012.
The reference program's roundings to bfloat16 on the way count: a program that leaves them out, or rounds other values in their place, can miss the bound.
Values may be sent and summed in bfloat16 or wider, within the bound.
A program may use at most 64 MiB of HBM per device.

```python
import math
import jax
import jax.numpy as jnp
from jax import lax

H = 1024
V = 100
K = 4
G_DEV = 512
N_DEV = 256
M = 8
NGRID = 32768
NODES = 16384


def draw_edge_index(key, part):
    key = jax.random.fold_in(key, 11)
    first_key, second_key = jax.random.split(key)
    band_id = jnp.arange(NGRID, dtype=jnp.int32) // G_DEV
    bands = NGRID // G_DEV
    lowest = jnp.where(band_id == 0, N_DEV, 0)
    highest = jnp.where(band_id == bands - 1, 2 * N_DEV, 3 * N_DEV)
    extent = highest - lowest
    offset = jax.random.randint(first_key, (NGRID,), 0, 1 << 20) % extent
    stride = 1 + jax.random.randint(second_key, (NGRID,), 0, 1 << 20) % (extent // 4 - 1)
    steps_k = jnp.arange(K, dtype=jnp.int32)
    return (lowest[:, None] + (offset[:, None] + steps_k[None, :] * stride[:, None]) % extent[:, None]).astype(jnp.int32)


def levels(own_key, shape, cuts, smallest, largest):
    factor_of = 1.0
    for axis_at, parts in cuts:
        draws = jax.random.uniform(jax.random.fold_in(jax.random.fold_in(own_key, 6), axis_at), (parts,), jnp.float32, smallest / len(cuts), largest / len(cuts))
        factor_of = factor_of * jnp.repeat(jnp.exp(draws), shape[axis_at] // parts).reshape((-1,) + (1,) * (len(shape) - 1 - axis_at))
    return factor_of


def noise(own_key, shape, width, limit, pieces=(), kind=jnp.bfloat16):
    entries = jax.random.normal(own_key, shape, jnp.float32) * width
    if len(pieces) > 0:
        entries = levels(own_key, shape, pieces, -0.22, 0.18) * entries
    return jnp.clip(entries, min=-limit, max=limit).astype(kind)


def setup_inputs(seed: int = 0) -> dict:
    arg_keys = jax.random.split(jax.random.key(seed), 7)
    latents = noise(arg_keys[0], (M, NODES, H), 1.0, 6.0, ((0, 4), (1, 64)))
    edge_index = draw_edge_index(jax.random.fold_in(arg_keys[6], 71), 0)
    edge_weight = jnp.clip(jnp.exp(math.log(1.0) - 2.3025851 * jax.random.uniform(arg_keys[2], (NGRID, K), jnp.float32) ** levels(arg_keys[2], (NGRID, K), ((0, 64),), -0.2, 0.2)), 0.1, 1.0)
    truth = noise(arg_keys[3], (V, NGRID), 1.0, 6.0, ((1, 64),), jnp.float32)
    w_hidden = noise(arg_keys[4], (H, H), H ** -0.5, 0.1875)
    output_weight = noise(arg_keys[5], (H, V), H ** -0.5, 0.1875)
    return dict(latents=latents, edge_index=edge_index, edge_weight=edge_weight, truth=truth, w_hidden=w_hidden, output_weight=output_weight)


smoothing = 0.05

def silu_slope(preact):
    logistic = jax.nn.sigmoid(preact)
    return logistic * (1.0 + preact * (1.0 - logistic))

def reference(latents, edge_index, edge_weight, truth, w_hidden, output_weight):
    loss_scale = 1.0 / math.sqrt(NGRID * M)
    padded = jnp.pad(latents, ((0, 0), (N_DEV, N_DEV), (0, 0)))
    rounded = lax.optimization_barrier(edge_weight.astype(jnp.bfloat16)).astype(jnp.float32)
    hidden_f = w_hidden.astype(jnp.float32)
    output_float = output_weight.astype(jnp.float32)

    def band_step(carry, band_id):
        grad_padded, grad_hid, grad_outw = carry
        node_start = (band_id * N_DEV).astype(jnp.int32)
        grid_start = (band_id * G_DEV).astype(jnp.int32)
        window = lax.dynamic_slice_in_dim(padded, node_start, 3 * N_DEV, 1)
        indices = lax.dynamic_slice_in_dim(edge_index, grid_start, G_DEV, 0)
        band_weights = lax.dynamic_slice_in_dim(rounded, grid_start, G_DEV, 0)
        observed_target = lax.dynamic_slice_in_dim(truth, grid_start, G_DEV, 1)
        gathered = window[:, indices, :].astype(jnp.float32)
        aggregate = jnp.einsum('mgkh,gk->mgh', gathered, band_weights).astype(jnp.bfloat16)
        preact = jnp.einsum('mgh,hk->mgk', aggregate.astype(jnp.float32), hidden_f)
        activation_values = jax.nn.silu(preact).astype(jnp.bfloat16)
        member_prediction = jnp.einsum('pak,kc->pca', activation_values.astype(jnp.float32), output_float)
        error_residual = member_prediction - observed_target[None]
        distance = jnp.sqrt(error_residual * error_residual + smoothing * smoothing)
        pairwise_distance = member_prediction[:, None] - member_prediction[None, :]
        ensemble_spread = lax.optimization_barrier(jnp.sum(pairwise_distance / jnp.sqrt(pairwise_distance * pairwise_distance + smoothing * smoothing), axis=1))
        dforecast = (loss_scale * (error_residual / (M * distance) - ensemble_spread / (M * (M - 1)))).astype(jnp.bfloat16)
        dforecast_f = dforecast.astype(jnp.float32)
        grad_outw = grad_outw + jnp.einsum('mgh,mvg->hv', activation_values.astype(jnp.float32), dforecast_f)
        dactivated = jnp.einsum('mvg,hv->mgh', dforecast_f, output_float)
        dpreact = (dactivated * silu_slope(preact)).astype(jnp.bfloat16)
        grad_hid = grad_hid + jnp.einsum('mgh,mgk->hk', aggregate.astype(jnp.float32), dpreact.astype(jnp.float32))
        daggregate = jnp.einsum('mgk,hk->mgh', dpreact.astype(jnp.float32), hidden_f).astype(jnp.bfloat16)
        contrib = jnp.einsum('mgh,gk->mgkh', daggregate.astype(jnp.float32), band_weights)
        grad_window = jnp.zeros((M, 3 * N_DEV, H), jnp.float32).at[:, indices.reshape(-1)].add(contrib.reshape(M, G_DEV * K, H))
        current = lax.dynamic_slice_in_dim(grad_padded, node_start, 3 * N_DEV, 1)
        grad_padded = lax.dynamic_update_slice_in_dim(grad_padded, current + grad_window, node_start, 1)
        return ((grad_padded, grad_hid, grad_outw), None)
    start = (jnp.zeros((M, NODES + 2 * N_DEV, H), jnp.float32), jnp.zeros((H, H), jnp.float32), jnp.zeros((H, V), jnp.float32))
    final, _ = lax.scan(band_step, start, jnp.arange(NGRID // G_DEV, dtype=jnp.int32))
    grad_padded, grad_hidden, grad_out = final
    return (grad_padded[:, N_DEV:N_DEV + NODES], grad_hidden, grad_out)
```

```python
import functools
import math

import jax
import jax.numpy as jnp
from jax import lax
from jax.experimental import pallas as pl
from jax.experimental.pallas import tpu as pltpu
from jax.sharding import PartitionSpec as P

MESH = pl.DeviceIdType.MESH
f32 = jnp.float32
bf16 = jnp.bfloat16
smoothing = 0.05

H = 1024
V = 100
VP = 128
NB = 256
G = 512
ENS = 4
NZ, NX = 8, 4
SPACE = NZ * NX * 2
QG = G // ENS
FC = 2
FW = H // FC
GC = 4
GW = H // GC
NJ = 2
ZJ = NZ // NJ


def mm(a, b):
    return jnp.dot(a, b, preferred_element_type=f32)


def cols(i, width):
    return pl.ds(pl.multiple_of(i * width, width), width)


def kernel(
    scale,
    lat, ei, ew, truth, w, wot,
    gl, gh, go,
    xw, at, a, wv, wt, wotr, wotv, wov, eiv, ewv, trr, trv, trt,
    aggc, aggt, pre, act, fcs, fcr, dfs, dfr, dfrt, dpre, daggc,
    low, up, rlow, rup, own,
    ghk, ghs, ghr, yk, ys, yr, xk, xs, xr, zr, ghv,
    gok, gos, gor, gzk, gzs, gzr, gxs, gxr, gyv, gyr,
    ld, fs, fr, es, er, bs, br, hs, hr, cs, cr, ysm, yrm, xsm, xrm, zsm, zrm, gsm, grm,
    gzsm, gzrm, gxsm, gxrm, gysm, gyrm, outsm,
):
    e = lax.axis_index("ens")
    s = lax.axis_index("space")
    z = s // 8
    x = (s // 2) % NX
    core = s % 2
    right = (e, (s + 1) % SPACE)
    left = (e, (s + SPACE - 1) % SPACE)
    mate = (e, z * 8 + x * 2 + (1 - core))
    ypeer = [((e + k) % ENS, s) for k in range(1, ENS)]
    xpeer = [(e, z * 8 + ((x + k) % NX) * 2 + core) for k in range(1, NX)]
    zpeer = [(e, ((z + k) % NZ) * 8 + x * 2 + core) for k in range(1, NZ)]

    def remote(src, dst, ssem, rsem, to):
        cp = pltpu.make_async_remote_copy(
            src_ref=src, dst_ref=dst, send_sem=ssem, recv_sem=rsem, device_id=to, device_id_type=MESH
        )
        sends.append(cp)
        return cp

    sends = []
    barrier = pltpu.get_barrier_semaphore()
    everyone = [left, right, mate] + ypeer + xpeer + zpeer
    for to in everyone:
        pl.semaphore_signal(barrier, inc=1, device_id=to, device_id_type=MESH)

    loads = [
        pltpu.make_async_copy(ei, eiv, ld.at[0]),
        pltpu.make_async_copy(ew, ewv, ld.at[1]),
        pltpu.make_async_copy(lat, xw.at[:, pl.ds(NB, NB)], ld.at[2]),
        pltpu.make_async_copy(w, wv, ld.at[3]),
        pltpu.make_async_copy(wot, wotr, ld.at[4]),
        pltpu.make_async_copy(truth.at[:, cols(e, QG)], trr, ld.at[5]),
    ]
    for cp in loads:
        cp.start()
    pl.semaphore_wait(barrier, len(everyone))

    halo = {}
    for m in range(2):
        for c in range(FC):
            i = m * FC + c
            part = lat.at[m, :, pl.ds(c * FW, FW)]
            up_cp = remote(part, xw.at[m, pl.ds(0, NB), pl.ds(c * FW, FW)], fs.at[0, i], fr.at[0, i], right)
            dn_cp = remote(part, xw.at[m, pl.ds(2 * NB, NB), pl.ds(c * FW, FW)], fs.at[1, i], fr.at[1, i], left)
            up_cp.start()
            dn_cp.start()
            halo[m, c] = (up_cp, dn_cp)

    loads[0].wait()
    loads[1].wait()
    wr = ewv[...].astype(bf16).astype(f32)

    @pl.loop(0, 3 * NB // 128)
    def _(b):
        row = lax.broadcasted_iota(jnp.int32, (128, G), 0) + b * 128
        t = jnp.zeros((128, G), f32)
        for k in range(4):
            t = jnp.where(row == eiv[pl.ds(k, 1), :], wr[k : k + 1, :], t)
        at[cols(b, 128), :] = t.astype(bf16)
        a[:, cols(b, 128)] = t.T.astype(bf16)

    loads[2].wait()
    loads[3].wait()

    @pl.loop(0, H // 128)
    def _(b):
        wt[:, cols(b, 128)] = wv[cols(b, 128), :].T

    loads[4].wait()
    loads[5].wait()
    wotv[...] = jnp.concatenate([wotr[...], jnp.zeros((VP - V, H), bf16)], axis=0)
    trv[...] = jnp.concatenate([trr[...], jnp.zeros((VP - V, QG), f32)], axis=0)
    wov[...] = wotv[...].T
    trt[...] = trv[...].T

    for m in range(2):
        for c in range(FC):
            for cp in halo[m, c]:
                cp.wait_recv()

            @pl.loop(0, FW // 256)
            def _(t):
                src = pl.ds(pl.multiple_of(c * FW + t * 256, 256), 256)
                part = mm(a[...], xw[m, :, src]).astype(bf16)
                aggc[:, cols(t, 256)] = part
                aggt[src, pl.ds(m * G, G)] = part.T

            @pl.loop(0, H // 256)
            def _(t):
                v = mm(aggc[...], wv[pl.ds(c * FW, FW), cols(t, 256)])
                if c > 0:
                    v = v + pre[m, :, cols(t, 256)]
                pre[m, :, cols(t, 256)] = v

        for k in range(ENS):
            r = (e + 1 + k) % ENS
            rows = cols(r, QG)

            @pl.loop(0, H // 256)
            def _(t):
                v = pre[m, rows, cols(t, 256)]
                sg = jax.nn.sigmoid(v)
                act[pl.ds(pl.multiple_of(m * G + r * QG, QG), QG), cols(t, 256)] = (v * sg).astype(bf16)
                pre[m, rows, cols(t, 256)] = sg * (1.0 + v * (1.0 - sg))

            fc = mm(act[pl.ds(pl.multiple_of(m * G + r * QG, QG), QG), :], wov[...])
            if k < ENS - 1:
                fcs[k, m] = fc
                remote(fcs.at[k, m], fcr.at[k, m], es.at[k, m], er.at[k, m], ypeer[k]).start()
            else:
                fcr[k, m] = fc

    for m in range(2):
        for k in range(ENS - 1):
            pltpu.make_async_remote_copy(
                src_ref=fcs.at[k, m], dst_ref=fcr.at[k, m], send_sem=es.at[k, m], recv_sem=er.at[k, m],
                device_id=ypeer[k], device_id_type=MESH,
            ).wait_recv()

    members = 2 * ENS

    @pl.loop(0, QG // 16)
    def _(b):
        rows = cols(b, 16)
        f = [fcr[i // 2, i % 2, rows, :] for i in range(members)]
        tr = trt[rows, :]
        total = [jnp.zeros((16, VP), f32) for _ in range(members)]
        for i in range(members):
            for j in range(i + 1, members):
                d = f[i] - f[j]
                q = d * lax.rsqrt(d * d + smoothing * smoothing)
                total[i] = total[i] + q
                total[j] = total[j] - q
        for i in range(members):
            d = f[i] - tr
            q = d * lax.rsqrt(d * d + smoothing * smoothing)
            dfs[i // 2, i % 2, rows, :] = (
                scale * (q * (1.0 / members) - total[i] * (1.0 / (members * (members - 1))))
            ).astype(bf16)

    for k in range(ENS - 1):
        back = ((e + ENS - 1 - k) % ENS, s)
        remote(dfs.at[k], dfr.at[:, cols(e, QG)], bs.at[k], br.at[k], back).start()
    dfr[:, cols(e, QG), :] = dfs[ENS - 1]
    for k in range(ENS - 1):
        src = (e + 1 + k) % ENS
        pltpu.make_async_remote_copy(
            src_ref=dfs.at[k], dst_ref=dfr.at[:, cols(src, QG)], send_sem=bs.at[k], recv_sem=br.at[k],
            device_id=((e + ENS - 1 - k) % ENS, s), device_id_type=MESH,
        ).wait_recv()

    def dpreact(m):
        @pl.loop(0, H // 256)
        def _(t):
            v = mm(dfr[m], wotv[:, cols(t, 256)])
            dpre[pl.ds(m * G, G), cols(t, 256)] = (v * pre[m, :, cols(t, 256)]).astype(bf16)

    grads = {}

    def node_grads(m, c):
        @pl.loop(0, GW // 256)
        def _(t):
            src = pl.ds(pl.multiple_of(c * GW + t * 256, 256), 256)
            daggc[...] = mm(dpre[pl.ds(m * G, G), :], wt[:, src]).astype(bf16)
            low[m, :, src] = mm(at[pl.ds(0, NB), :], daggc[...]).astype(bf16)
            up[m, :, src] = mm(at[pl.ds(2 * NB, NB), :], daggc[...]).astype(bf16)
            own[m, :, src] = mm(at[pl.ds(NB, NB), :], daggc[...])

        i = m * GC + c
        part = pl.ds(c * GW, GW)
        one = remote(low.at[m, :, part], rlow.at[m, :, part], hs.at[0, i], hr.at[0, i], left)
        two = remote(up.at[m, :, part], rup.at[m, :, part], hs.at[1, i], hr.at[1, i], right)
        one.start()
        two.start()
        grads[m, c] = (one, two)

    dpreact(0)
    for c in range(GC):
        node_grads(0, c)
    dpreact(1)

    for m in range(2):
        dfrt[:, pl.ds(m * G, G)] = dfr[m].T

    @pl.loop(0, H // 256)
    def _(t):
        v = mm(dfrt[...], act[:, cols(t, 256)]).T
        v = v.reshape(256 // 32, 2, 16, VP)
        mine = jnp.where(core == 0, v[:, 0], v[:, 1])
        other = jnp.where(core == 0, v[:, 1], v[:, 0])
        gok[cols(t, 8)] = mine
        gos[cols(t, 8)] = other.astype(bf16)

    gcp = remote(gos, gor, gsm.at[0], grm.at[0], mate)
    gcp.start()

    RJ = H // NJ
    gcore = []
    for j in range(NJ):
        @pl.loop(0, (RJ // 256) * (H // 256))
        def _(t):
            rb = t // (H // 256)
            cb = t % (H // 256)
            v = mm(aggt[pl.ds(pl.multiple_of(j * RJ + rb * 256, 256), 256), :], dpre[:, cols(cb, 256)])
            v = v.reshape(256 // 32, 2, 16, 256)
            groups = pl.ds(j * (RJ // 32) + rb * 8, 8)
            ghk[groups, :, cols(cb, 256)] = jnp.where(core == 0, v[:, 0], v[:, 1])
            ghs[groups, :, cols(cb, 256)] = jnp.where(core == 0, v[:, 1], v[:, 0]).astype(bf16)

        half = pl.ds(j * (RJ // 32), RJ // 32)
        cp = remote(ghs.at[half], ghr.at[half], cs.at[j], cr.at[j], mate)
        cp.start()
        gcore.append(cp)

    gcp.wait_recv()
    gzs[...] = (gok[...] + gor[...].astype(f32)).astype(bf16)
    gz = []
    for k in range(1, NZ):
        cp = remote(gzs.at[cols((z + k) % NZ, NX)], gzr.at[k - 1], gzsm.at[k - 1], gzrm.at[k - 1], zpeer[k - 1])
        cp.start()
        gz.append(cp)
    gzk[...] = gok[cols(z, NX)] + gor[cols(z, NX)].astype(f32)

    ycp = []
    QC = H // ENS
    for j in range(NJ):
        gcore[j].wait_recv()
        NG = RJ // 32

        @pl.loop(0, NG // 4)
        def _(t):
            groups = pl.ds(j * NG + t * 4, 4)
            v = ghk[groups] + ghr[groups].astype(f32)
            ghk[groups] = v
            ys[groups] = v.astype(bf16)

        half = pl.ds(j * NG, NG)
        for k in range(1, ENS):
            cp = remote(
                ys.at[half, :, cols((e + k) % ENS, QC)], yr.at[k - 1, half], ysm.at[k - 1, j], yrm.at[k - 1, j],
                ypeer[k - 1],
            )
            cp.start()
            ycp.append(cp)

    for c in range(GC):
        node_grads(1, c)

    for cp in gz:
        cp.wait_recv()
    v = gzk[...]
    for k in range(NZ - 1):
        v = v + gzr[k].astype(f32)
    gzk[...] = v
    gxs[...] = v.astype(bf16)
    gx = []
    for k in range(1, NX):
        cp = remote(gxs.at[(x + k) % NX], gxr.at[k - 1], gxsm.at[k - 1], gxrm.at[k - 1], xpeer[k - 1])
        cp.start()
        gx.append(cp)

    outs = []
    for m in range(2):
        for c in range(GC):
            for cp in grads[m, c]:
                cp.wait_recv()
            part = pl.ds(c * GW, GW)
            own[m, :, part] = own[m, :, part] + rlow[m, :, part].astype(f32) + rup[m, :, part].astype(f32)
            cp = pltpu.make_async_copy(own.at[m, :, part], gl.at[m, :, part], outsm.at[m * GC + c])
            cp.start()
            outs.append(cp)

    xcp = []
    for j in range(NJ):
        for k in range(ENS - 1):
            ycp[j * (ENS - 1) + k].wait_recv()
        NG = RJ // 32
        half = pl.ds(j * NG, NG)
        v = ghk[half, :, cols(e, QC)]
        for k in range(ENS - 1):
            v = v + yr[k, half].astype(f32)
        zz = pl.ds(j * ZJ, ZJ)
        xk[zz] = v.reshape(ZJ, NX, 16, QC)
        xs[zz] = v.reshape(ZJ, NX, 16, QC).astype(bf16)
        for k in range(1, NX):
            cp = remote(
                xs.at[zz, (x + k) % NX], xr.at[k - 1, zz], xsm.at[k - 1, j], xrm.at[k - 1, j], xpeer[k - 1]
            )
            cp.start()
            xcp.append(cp)

    for cp in gx:
        cp.wait_recv()
    v = gzk[x]
    for k in range(NX - 1):
        v = v + gxr[k].astype(f32)
    gyv[...] = v
    gy = []
    for k in range(1, ENS):
        cp = remote(gyv, gyr.at[k - 1], gysm.at[k - 1], gyrm.at[k - 1], ypeer[k - 1])
        cp.start()
        gy.append(cp)

    for j in range(NJ):
        for k in range(NX - 1):
            xcp[j * (NX - 1) + k].wait_recv()
        zz = pl.ds(j * ZJ, ZJ)
        v = xk[zz, x]
        for k in range(NX - 1):
            v = v + xr[k, zz].astype(f32)
        xk[zz, x] = v
    zcp = []
    for k in range(1, NZ):
        cp = remote(xk.at[(z + k) % NZ, x], zr.at[k - 1], zsm.at[k - 1], zrm.at[k - 1], zpeer[k - 1])
        cp.start()
        zcp.append(cp)
    for cp in zcp:
        cp.wait_recv()
    v = xk[z, x]
    for k in range(NZ - 1):
        v = v + zr[k]
    ghv[:, cols(e, QC)] = v
    last = []
    for k in range(1, ENS):
        mine = ghv.at[:, cols(e, QC)]
        cp = remote(mine, mine, gsm.at[k], grm.at[k], ypeer[k - 1])
        cp.start()
    for cp in gy:
        cp.wait_recv()
    v = gyv[...]
    for k in range(ENS - 1):
        v = v + gyr[k]
    go[...] = v[:, :V]
    for k in range(1, ENS):
        src = (e + ENS - k) % ENS
        theirs = ghv.at[:, cols(src, QC)]
        pltpu.make_async_remote_copy(
            src_ref=theirs, dst_ref=theirs, send_sem=gsm.at[k], recv_sem=grm.at[k],
            device_id=ypeer[k - 1], device_id_type=MESH,
        ).wait_recv()
    gh[...] = ghv[...]
    for cp in outs:
        cp.wait()
    for cp in sends:
        cp.wait_send()


def shards(latents, edge_index, edge_weight, truth, w_hidden, output_weight):
    members = latents.shape[0] * lax.axis_size("ens")
    cells = truth.shape[1] * lax.axis_size("space")
    scale = 1.0 / math.sqrt(cells * members)
    any_ = pl.BlockSpec(memory_space=pl.ANY)
    vm = pl.BlockSpec(memory_space=pltpu.VMEM)
    dma = pltpu.SemaphoreType.DMA
    R2 = H // 32
    QC = H // ENS
    scratch = [
        pltpu.VMEM((2, 3 * NB, H), bf16),
        pltpu.VMEM((3 * NB, G), bf16),
        pltpu.VMEM((G, 3 * NB), bf16),
        pltpu.VMEM((H, H), bf16),
        pltpu.VMEM((H, H), bf16),
        pltpu.VMEM((V, H), bf16),
        pltpu.VMEM((VP, H), bf16),
        pltpu.VMEM((H, VP), bf16),
        pltpu.VMEM((4, G), jnp.int32),
        pltpu.VMEM((4, G), f32),
        pltpu.VMEM((V, QG), f32),
        pltpu.VMEM((VP, QG), f32),
        pltpu.VMEM((QG, VP), f32),
        pltpu.VMEM((G, FW), bf16),
        pltpu.VMEM((H, 2 * G), bf16),
        pltpu.VMEM((2, G, H), f32),
        pltpu.VMEM((2 * G, H), bf16),
        pltpu.VMEM((ENS - 1, 2, QG, VP), f32),
        pltpu.VMEM((ENS, 2, QG, VP), f32),
        pltpu.VMEM((ENS, 2, QG, VP), bf16),
        pltpu.VMEM((2, G, VP), bf16),
        pltpu.VMEM((VP, 2 * G), bf16),
        pltpu.VMEM((2 * G, H), bf16),
        pltpu.VMEM((G, 256), bf16),
        pltpu.VMEM((2, NB, H), bf16),
        pltpu.VMEM((2, NB, H), bf16),
        pltpu.VMEM((2, NB, H), bf16),
        pltpu.VMEM((2, NB, H), bf16),
        pltpu.VMEM((2, NB, H), f32),
        pltpu.VMEM((R2, 16, H), f32),
        pltpu.VMEM((R2, 16, H), bf16),
        pltpu.VMEM((R2, 16, H), bf16),
        pltpu.VMEM((8, 128), f32),
        pltpu.VMEM((R2, 16, H), bf16),
        pltpu.VMEM((ENS - 1, R2, 16, QC), bf16),
        pltpu.VMEM((NZ, NX, 16, QC), f32),
        pltpu.VMEM((NZ, NX, 16, QC), bf16),
        pltpu.VMEM((NX - 1, NZ, 16, QC), bf16),
        pltpu.VMEM((NZ - 1, 16, QC), f32),
        pltpu.VMEM((16, H), f32),
        pltpu.VMEM((R2, 16, VP), f32),
        pltpu.VMEM((R2, 16, VP), bf16),
        pltpu.VMEM((R2, 16, VP), bf16),
        pltpu.VMEM((NX, 16, VP), f32),
        pltpu.VMEM((R2, 16, VP), bf16),
        pltpu.VMEM((NZ - 1, NX, 16, VP), bf16),
        pltpu.VMEM((NX, 16, VP), bf16),
        pltpu.VMEM((NX - 1, 16, VP), bf16),
        pltpu.VMEM((16, VP), f32),
        pltpu.VMEM((ENS - 1, 16, VP), f32),
        dma((6,)),
        dma((2, 2 * FC)), dma((2, 2 * FC)),
        dma((ENS - 1, 2)), dma((ENS - 1, 2)),
        dma((ENS - 1,)), dma((ENS - 1,)),
        dma((2, 2 * GC)), dma((2, 2 * GC)),
        dma((NJ,)), dma((NJ,)),
        dma((ENS - 1, NJ)), dma((ENS - 1, NJ)),
        dma((NX - 1, NJ)), dma((NX - 1, NJ)),
        dma((NZ - 1,)), dma((NZ - 1,)),
        dma((ENS,)), dma((ENS,)),
        dma((NZ - 1,)), dma((NZ - 1,)),
        dma((NX - 1,)), dma((NX - 1,)),
        dma((ENS - 1,)), dma((ENS - 1,)),
        dma((2 * GC,)),
    ]
    return pl.pallas_call(
        functools.partial(kernel, scale),
        out_shape=(
            jax.ShapeDtypeStruct((2, NB, H), f32),
            jax.ShapeDtypeStruct((16, H), f32),
            jax.ShapeDtypeStruct((16, V), f32),
        ),
        in_specs=[any_] * 6,
        out_specs=(any_, vm, vm),
        scratch_shapes=scratch,
        compiler_params=pltpu.CompilerParams(
            collective_id=0, has_side_effects=True, vmem_limit_bytes=56 << 20
        ),
        name="decoder",
    )(latents, edge_index.T, edge_weight.T, truth, w_hidden, output_weight.T)


def solution(mesh):
    placed = (
        P("ens", "space", None),
        P("space", None),
        P("space", None),
        P(None, "space"),
        P(),
        P(),
    )
    return jax.shard_map(
        shards,
        mesh=mesh,
        in_specs=placed,
        out_specs=(P("ens", "space", None), P("space", None), P("space", None)),
        check_vma=False,
    )
```

```python
import functools
import math

import jax
import jax.numpy as jnp
from jax import lax
from jax.experimental import pallas as pl
from jax.experimental.pallas import tpu as pltpu
from jax.sharding import PartitionSpec as P

MESH = pl.DeviceIdType.MESH
f32 = jnp.float32
bf16 = jnp.bfloat16
smoothing = 0.05

H = 1024
V = 100
VP = 128
NB = 256
G = 512
ENS = 4
NZ, NX = 8, 4
SPACE = NZ * NX * 2
QG = G // ENS
QC = H // ENS
VS = 104
VM = 112
NJ = 2
LAG = 1
ZJ = NZ // NJ
PIECES = ((0, 0, 512), (0, 512, 512), (1, 0, 512), (1, 512, 256), (1, 768, 256))
AHEAD = 3
VLIM = 56
CUTS = 8
GPIECES = ((0, 0, 512), (0, 512, 512), (1, 0, 512), (1, 512, 512))


def mm(a, b):
    return jnp.dot(a, b, preferred_element_type=f32)


def cols(i, width):
    return pl.ds(pl.multiple_of(i * width, width), width)


def nt(a, b):
    return lax.dot_general(a, b, (((1,), (1,)), ((), ())), preferred_element_type=f32)


def tn(a, b):
    return lax.dot_general(a, b, (((0,), (0,)), ((), ())), preferred_element_type=f32)


def kernel(
    scale,
    lat, ei, ew, truth, w, wot,
    gl, gh, go,
    xw, at, a, wv, wotr, wotv, eiv, ewv, trr, trv,
    agg, pre, act, fcs, fcr, dfs, dfr, dpre, daggc,
    low, up, rlow, rup, own,
    ghk, ghs, ghr, ys, yr, xk, xs, xr, zs, zr, ghv,
    gok, gos, gor, gzk, gzs, gzr, gxs, gxr, gyv, gyr,
    ld, fs, fr, es, er, bs, br, hs, hr, cs, cr, ysm, yrm, xsm, xrm, zsm, zrm, gsm, grm,
    gzsm, gzrm, gxsm, gxrm, gysm, gyrm, outsm,
):
    e = lax.axis_index("ens")
    s = lax.axis_index("space")
    z = s // 8
    x = (s // 2) % NX
    core = s % 2
    right = (e, (s + 1) % SPACE)
    left = (e, (s + SPACE - 1) % SPACE)
    mate = (e, z * 8 + x * 2 + (1 - core))
    ypeer = [((e + k) % ENS, s) for k in range(1, ENS)]
    xpeer = [(e, z * 8 + ((x + k) % NX) * 2 + core) for k in range(1, NX)]
    zpeer = [(e, ((z + k) % NZ) * 8 + x * 2 + core) for k in range(1, NZ)]

    def remote(src, dst, ssem, rsem, to):
        cp = pltpu.make_async_remote_copy(
            src_ref=src, dst_ref=dst, send_sem=ssem, recv_sem=rsem, device_id=to, device_id_type=MESH
        )
        sends.append(cp)
        return cp

    sends = []
    barrier = pltpu.get_barrier_semaphore()
    everyone = [left, right, mate] + ypeer + xpeer + zpeer
    for to in everyone:
        pl.semaphore_signal(barrier, inc=1, device_id=to, device_id_type=MESH)

    loads = [
        pltpu.make_async_copy(ei, eiv, ld.at[0]),
        pltpu.make_async_copy(ew, ewv, ld.at[1]),
        pltpu.make_async_copy(lat, xw.at[:, pl.ds(NB, NB)], ld.at[2]),
        pltpu.make_async_copy(w, wv, ld.at[3]),
        pltpu.make_async_copy(wot, wotr, ld.at[4]),
        pltpu.make_async_copy(truth.at[:, cols(e, QG)], trr, ld.at[5]),
    ]
    for cp in loads:
        cp.start()
    pl.semaphore_wait(barrier, len(everyone))

    halo = {}

    def send_halo(i):
        m, first, width = PIECES[i]
        part = lat.at[m, :, pl.ds(first, width)]
        up_cp = remote(part, xw.at[m, pl.ds(0, NB), pl.ds(first, width)], fs.at[0, i], fr.at[0, i], right)
        dn_cp = remote(part, xw.at[m, pl.ds(2 * NB, NB), pl.ds(first, width)], fs.at[1, i], fr.at[1, i], left)
        up_cp.start()
        dn_cp.start()
        halo[i] = (up_cp, dn_cp)

    for i in range(AHEAD):
        send_halo(i)

    loads[0].wait()
    loads[1].wait()
    wr = ewv[...].astype(bf16).astype(f32)

    @pl.loop(0, 3 * NB // 128)
    def _(b):
        row = lax.broadcasted_iota(jnp.int32, (128, G), 0) + b * 128
        t = jnp.zeros((128, G), f32)
        for k in range(4):
            t = jnp.where(row == eiv[pl.ds(k, 1), :], wr[k : k + 1, :], t)
        at[cols(b, 128), :] = t.astype(bf16)
        a[:, cols(b, 128)] = t.T.astype(bf16)

    for cp in loads[2:]:
        cp.wait()
    wotv[...] = jnp.concatenate([wotr[...], jnp.zeros((VP - V, H), bf16)], axis=0)
    trv[...] = jnp.concatenate([trr[...], jnp.zeros((VM - V, QG), f32)], axis=0)
    for k in range(ENS):
        for m in range(2):
            fcr[k, m, pl.ds(VS, VM - VS), :] = jnp.zeros((VM - VS, QG), f32)
    for m in range(2):
        dfr[m, pl.ds(VM, VP - VM), :] = jnp.zeros((VP - VM, G), bf16)

    def slope(m):
        @pl.loop(0, H // 256)
        def _(t):
            v = pre[m, :, cols(t, 256)]
            sg = jax.nn.sigmoid(v)
            pre[m, :, cols(t, 256)] = sg * (1.0 + v * (1.0 - sg))

    for i, (m, first, width) in enumerate(PIECES):
        for cp in halo[i]:
            cp.wait_recv()
        if i + AHEAD < len(PIECES):
            send_halo(i + AHEAD)
        part = pl.ds(first, width)
        agg[pl.ds(m * G, G), part] = mm(a[...], xw[m, :, part]).astype(bf16)
        v = mm(agg[pl.ds(m * G, G), part], wv[part, :])
        if first > 0:
            v = v + pre[m]
        pre[m] = v
        if first + width < H:
            continue
        for k in range(ENS):
            r = (e + 1 + k) % ENS
            rows = cols(r, QG)
            arows = pl.ds(pl.multiple_of(m * G + r * QG, QG), QG)
            v = pre[m, rows, :]
            act[arows, :] = (v * jax.nn.sigmoid(v)).astype(bf16)
            fc = nt(wotv[pl.ds(0, VM), :], act[arows, :])
            if k < ENS - 1:
                fcs[k, m] = fc[:VS]
                remote(
                    fcs.at[k, m], fcr.at[k, m, pl.ds(0, VS)], es.at[k, m], er.at[k, m], ypeer[k]
                ).start()
            else:
                fcr[k, m, pl.ds(0, VS), :] = fc[:VS]
        slope(m)

    for m in range(2):
        for k in range(ENS - 1):
            pltpu.make_async_remote_copy(
                src_ref=fcs.at[k, m], dst_ref=fcr.at[k, m, pl.ds(0, VS)], send_sem=es.at[k, m],
                recv_sem=er.at[k, m], device_id=ypeer[k], device_id_type=MESH,
            ).wait_recv()

    members = 2 * ENS

    @pl.loop(0, VM // 16)
    def _(b):
        rows = cols(b, 16)
        f = [fcr[i // 2, i % 2, rows, :] for i in range(members)]
        tr = trv[rows, :]
        total = [jnp.zeros((16, QG), f32) for _ in range(members)]
        for i in range(members):
            for j in range(i + 1, members):
                d = f[i] - f[j]
                q = d * lax.rsqrt(d * d + smoothing * smoothing)
                total[i] = total[i] + q
                total[j] = total[j] - q
        for i in range(members):
            d = f[i] - tr
            q = d * lax.rsqrt(d * d + smoothing * smoothing)
            dfs[i // 2, i % 2, rows, :] = (
                scale * (q * (1.0 / members) - total[i] * (1.0 / (members * (members - 1))))
            ).astype(bf16)

    for k in range(ENS - 1):
        back = ((e + ENS - 1 - k) % ENS, s)
        remote(dfs.at[k], dfr.at[:, pl.ds(0, VM), cols(e, QG)], bs.at[k], br.at[k], back).start()
    dfr[:, pl.ds(0, VM), cols(e, QG)] = dfs[ENS - 1]
    for k in range(ENS - 1):
        src = (e + 1 + k) % ENS
        pltpu.make_async_remote_copy(
            src_ref=dfs.at[k], dst_ref=dfr.at[:, pl.ds(0, VM), cols(src, QG)], send_sem=bs.at[k],
            recv_sem=br.at[k], device_id=((e + ENS - 1 - k) % ENS, s), device_id_type=MESH,
        ).wait_recv()

    for m in range(2):
        dpre[pl.ds(m * G, G), :] = (tn(dfr[m], wotv[...]) * pre[m]).astype(bf16)

    RJ = H // NJ
    NG = RJ // 32
    gcore = []
    ycp = []

    def send_y(j):
        gcore[j].wait_recv()
        groups = pl.ds(j * NG, NG)
        v = ghk[groups] + ghr[groups].astype(f32)
        ghk[groups] = v
        for k in range(ENS):
            ys[k, groups] = v[:, :, k * QC : (k + 1) * QC].astype(bf16)
        for k in range(1, ENS):
            cp = remote(
                ys.at[(e + k) % ENS, groups], yr.at[k - 1, groups], ysm.at[k - 1, j],
                yrm.at[k - 1, j], ypeer[k - 1],
            )
            cp.start()
            ycp.append(cp)

    grads = []

    def node_grads(i):
        m, first, width = GPIECES[i]
        part = pl.ds(first, width)
        daggc[:, pl.ds(0, width)] = nt(dpre[pl.ds(m * G, G), :], wv[part, :]).astype(bf16)
        v = mm(at[...], daggc[:, pl.ds(0, width)])
        low[i] = v[:NB].astype(bf16)
        up[i] = v[2 * NB :].astype(bf16)
        own[m, :, part] = v[NB : 2 * NB]
        one = remote(low.at[i], rlow.at[i], hs.at[0, i], hr.at[0, i], left)
        two = remote(up.at[i], rup.at[i], hs.at[1, i], hr.at[1, i], right)
        one.start()
        two.start()
        grads.append((one, two))

    node_grads(0)
    node_grads(1)
    for j in range(NJ):
        v = tn(agg[:, pl.ds(j * RJ, RJ)], dpre[...]).reshape(NG, 2, 16, H)
        groups = pl.ds(j * NG, NG)
        ghk[groups] = jnp.where(core == 0, v[:, 0], v[:, 1])
        ghs[groups] = jnp.where(core == 0, v[:, 1], v[:, 0]).astype(bf16)
        cp = remote(ghs.at[groups], ghr.at[groups], cs.at[j], cr.at[j], mate)
        cp.start()
        gcore.append(cp)
        if j >= LAG:
            send_y(j - LAG)
    node_grads(2)
    for j in range(NJ - LAG, NJ):
        send_y(j)
    for i in range(3, len(GPIECES)):
        node_grads(i)

    v = mm(dfr[0], act[pl.ds(0, G), :]) + mm(dfr[1], act[pl.ds(G, G), :])
    v = v.T.reshape(H // 32, 2, 16, VP)
    gok[...] = jnp.where(core == 0, v[:, 0], v[:, 1])
    gos[...] = jnp.where(core == 0, v[:, 1], v[:, 0]).astype(bf16)
    gcp = remote(gos, gor, gsm.at[0], grm.at[0], mate)
    gcp.start()
    gcp.wait_recv()
    gzs[...] = (gok[...] + gor[...].astype(f32)).astype(bf16)
    gz = []
    for k in range(1, NZ):
        cp = remote(gzs.at[cols((z + k) % NZ, NX)], gzr.at[k - 1], gzsm.at[k - 1], gzrm.at[k - 1], zpeer[k - 1])
        cp.start()
        gz.append(cp)
    gzk[...] = gok[cols(z, NX)] + gor[cols(z, NX)].astype(f32)

    for cp in gz:
        cp.wait_recv()
    v = gzk[...]
    for k in range(NZ - 1):
        v = v + gzr[k].astype(f32)
    gzk[...] = v
    gxs[...] = v.astype(bf16)
    gx = []
    for k in range(1, NX):
        cp = remote(gxs.at[(x + k) % NX], gxr.at[k - 1], gxsm.at[k - 1], gxrm.at[k - 1], xpeer[k - 1])
        cp.start()
        gx.append(cp)

    xcp = []

    def send_x(j):
        for k in range(ENS - 1):
            ycp[j * (ENS - 1) + k].wait_recv()
        groups = pl.ds(j * NG, NG)
        v = ghk[groups, :, cols(e, QC)]
        for k in range(ENS - 1):
            v = v + yr[k, groups].astype(f32)
        zz = pl.ds(j * ZJ, ZJ)
        xk[zz] = v.reshape(ZJ, NX, 16, QC)
        for k in range(NX):
            xs[k, zz] = xk[zz, k].astype(bf16)
        for k in range(1, NX):
            cp = remote(
                xs.at[(x + k) % NX, zz], xr.at[k - 1, zz], xsm.at[k - 1, j], xrm.at[k - 1, j], xpeer[k - 1]
            )
            cp.start()
            xcp.append(cp)

    def add_x(j):
        for k in range(NX - 1):
            xcp[j * (NX - 1) + k].wait_recv()
        zz = pl.ds(j * ZJ, ZJ)
        v = xk[zz, x]
        for k in range(NX - 1):
            v = v + xr[k, zz].astype(f32)
        xk[zz, x] = v
        zs[zz] = v.astype(bf16)

    outs = []

    def finish(i):
        m, first, width = GPIECES[i]
        for cp in grads[i]:
            cp.wait_recv()
        part = pl.ds(first, width)
        own[m, :, part] = own[m, :, part] + rlow[i].astype(f32) + rup[i].astype(f32)
        cp = pltpu.make_async_copy(own.at[m, :, part], gl.at[m, :, part], outsm.at[i])
        cp.start()
        outs.append(cp)

    left_over = list(range(len(GPIECES)))
    for j in range(NJ):
        send_x(j)
        if j >= 1:
            add_x(j - 1)
        if j < NJ - 1:
            finish(left_over.pop(0))

    for cp in gx:
        cp.wait_recv()
    v = gzk[x]
    for k in range(NX - 1):
        v = v + gxr[k].astype(f32)
    gyv[...] = v
    gy = []
    for k in range(1, ENS):
        cp = remote(gyv, gyr.at[k - 1], gysm.at[k - 1], gyrm.at[k - 1], ypeer[k - 1])
        cp.start()
        gy.append(cp)

    add_x(NJ - 1)
    zcp = []
    for k in range(1, NZ):
        cp = remote(zs.at[(z + k) % NZ], zr.at[k - 1], zsm.at[k - 1], zrm.at[k - 1], zpeer[k - 1])
        cp.start()
        zcp.append(cp)
    for i in left_over:
        finish(i)
    for cp in gy:
        cp.wait_recv()
    v = gyv[...]
    for k in range(ENS - 1):
        v = v + gyr[k]
    go[...] = v[:, :V]
    for cp in zcp:
        cp.wait_recv()
    v = xk[z, x]
    for k in range(NZ - 1):
        v = v + zr[k].astype(f32)
    ghv[:, cols(e, QC)] = v
    for k in range(1, ENS):
        mine = ghv.at[:, cols(e, QC)]
        remote(mine, mine, gsm.at[k], grm.at[k], ypeer[k - 1]).start()
    for k in range(1, ENS):
        src = (e + ENS - k) % ENS
        theirs = ghv.at[:, cols(src, QC)]
        pltpu.make_async_remote_copy(
            src_ref=theirs, dst_ref=theirs, send_sem=gsm.at[k], recv_sem=grm.at[k],
            device_id=ypeer[k - 1], device_id_type=MESH,
        ).wait_recv()
    gh[...] = ghv[...]
    for cp in outs:
        cp.wait()
    for cp in sends:
        cp.wait_send()


def hand_over(a, b, c, oa, ob, oc, va, vb, vc, isem, osem):
    rows = a.shape[1] // CUTS * 2
    places = [(i % 2, pl.ds(i // 2 * rows, rows)) for i in range(CUTS)]
    moves = [(a.at[p], va.at[p], oa.at[p]) for p in places] + [(b, vb, ob), (c, vc, oc)]
    ins = [pltpu.make_async_copy(src, mid, isem.at[i]) for i, (src, mid, _) in enumerate(moves)]
    outs = [pltpu.make_async_copy(mid, dst, osem.at[i]) for i, (_, mid, dst) in enumerate(moves)]
    for cp in ins:
        cp.start()
    for one, two in zip(ins, outs):
        one.wait()
        two.start()
    for cp in outs:
        cp.wait()


def shards(latents, edge_index, edge_weight, truth, w_hidden, output_weight):
    members = latents.shape[0] * lax.axis_size("ens")
    cells = truth.shape[1] * lax.axis_size("space")
    scale = 1.0 / math.sqrt(cells * members)
    any_ = pl.BlockSpec(memory_space=pl.ANY)
    vm = pl.BlockSpec(memory_space=pltpu.VMEM)
    dma = pltpu.SemaphoreType.DMA
    R2 = H // 32
    scratch = [
        pltpu.VMEM((2, 3 * NB, H), bf16),
        pltpu.VMEM((3 * NB, G), bf16),
        pltpu.VMEM((G, 3 * NB), bf16),
        pltpu.VMEM((H, H), bf16),
        pltpu.VMEM((V, H), bf16),
        pltpu.VMEM((VP, H), bf16),
        pltpu.VMEM((4, G), jnp.int32),
        pltpu.VMEM((4, G), f32),
        pltpu.VMEM((V, QG), f32),
        pltpu.VMEM((VM, QG), f32),
        pltpu.VMEM((2 * G, H), bf16),
        pltpu.VMEM((2, G, H), f32),
        pltpu.VMEM((2 * G, H), bf16),
        pltpu.VMEM((ENS - 1, 2, VS, QG), f32),
        pltpu.VMEM((ENS, 2, VM, QG), f32),
        pltpu.VMEM((ENS, 2, VM, QG), bf16),
        pltpu.VMEM((2, VP, G), bf16),
        pltpu.VMEM((2 * G, H), bf16),
        pltpu.VMEM((G, 512), bf16),
        pltpu.VMEM((len(GPIECES), NB, 512), bf16),
        pltpu.VMEM((len(GPIECES), NB, 512), bf16),
        pltpu.VMEM((len(GPIECES), NB, 512), bf16),
        pltpu.VMEM((len(GPIECES), NB, 512), bf16),
        pltpu.VMEM((2, NB, H), f32),
        pltpu.VMEM((R2, 16, H), f32),
        pltpu.VMEM((R2, 16, H), bf16),
        pltpu.VMEM((R2, 16, H), bf16),
        pltpu.VMEM((ENS, R2, 16, QC), bf16),
        pltpu.VMEM((ENS - 1, R2, 16, QC), bf16),
        pltpu.VMEM((NZ, NX, 16, QC), f32),
        pltpu.VMEM((NX, NZ, 16, QC), bf16),
        pltpu.VMEM((NX - 1, NZ, 16, QC), bf16),
        pltpu.VMEM((NZ, 16, QC), bf16),
        pltpu.VMEM((NZ - 1, 16, QC), bf16),
        pltpu.VMEM((16, H), f32),
        pltpu.VMEM((R2, 16, VP), f32),
        pltpu.VMEM((R2, 16, VP), bf16),
        pltpu.VMEM((R2, 16, VP), bf16),
        pltpu.VMEM((NX, 16, VP), f32),
        pltpu.VMEM((R2, 16, VP), bf16),
        pltpu.VMEM((NZ - 1, NX, 16, VP), bf16),
        pltpu.VMEM((NX, 16, VP), bf16),
        pltpu.VMEM((NX - 1, 16, VP), bf16),
        pltpu.VMEM((16, VP), f32),
        pltpu.VMEM((ENS - 1, 16, VP), f32),
        dma((6,)),
        dma((2, len(PIECES))), dma((2, len(PIECES))),
        dma((ENS - 1, 2)), dma((ENS - 1, 2)),
        dma((ENS - 1,)), dma((ENS - 1,)),
        dma((2, len(GPIECES))), dma((2, len(GPIECES))),
        dma((NJ,)), dma((NJ,)),
        dma((ENS - 1, NJ)), dma((ENS - 1, NJ)),
        dma((NX - 1, NJ)), dma((NX - 1, NJ)),
        dma((NZ - 1,)), dma((NZ - 1,)),
        dma((ENS,)), dma((ENS,)),
        dma((NZ - 1,)), dma((NZ - 1,)),
        dma((NX - 1,)), dma((NX - 1,)),
        dma((ENS - 1,)), dma((ENS - 1,)),
        dma((len(GPIECES),)),
    ]
    held = pl.pallas_call(
        functools.partial(kernel, scale),
        out_shape=(
            jax.ShapeDtypeStruct((2, NB, H), f32),
            jax.ShapeDtypeStruct((16, H), f32),
            jax.ShapeDtypeStruct((16, V), f32),
        ),
        in_specs=[any_] * 6,
        out_specs=(any_, vm, vm),
        scratch_shapes=scratch,
        compiler_params=pltpu.CompilerParams(
            collective_id=0, has_side_effects=True, vmem_limit_bytes=VLIM << 20
        ),
        name="decoder",
    )(latents, edge_index.T, edge_weight.T, truth, w_hidden, output_weight.T)
    return pl.pallas_call(
        hand_over,
        out_shape=[jax.ShapeDtypeStruct(v.shape, v.dtype) for v in held],
        in_specs=[any_] * 3,
        out_specs=[any_] * 3,
        scratch_shapes=[pltpu.VMEM(v.shape, v.dtype) for v in held] + [dma((CUTS + 2,)), dma((CUTS + 2,))],
        name="hand_over",
    )(*held)


def solution(mesh):
    placed = (
        P("ens", "space", None),
        P("space", None),
        P("space", None),
        P(None, "space"),
        P(),
        P(),
    )
    return jax.shard_map(
        shards,
        mesh=mesh,
        in_specs=placed,
        out_specs=(P("ens", "space", None), P("space", None), P("space", None)),
        check_vma=False,
    )
```

```python
import functools
import math

import jax
import jax.numpy as jnp
from jax import lax
from jax.experimental import pallas as pl
from jax.experimental.pallas import tpu as pltpu
from jax.sharding import PartitionSpec as P

MESH = pl.DeviceIdType.MESH
f32 = jnp.float32
bf16 = jnp.bfloat16
smoothing = 0.05

H = 1024
V = 100
VP = 128
NB = 256
G = 512
ENS = 4
NZ, NX = 8, 4
SPACE = NZ * NX * 2
QG = G // ENS
QC = H // ENS
VS = 104
VM = 112
NJ = 2
LAG = 1
ZJ = NZ // NJ
PIECES = ((0, 0, 512), (0, 512, 512), (1, 0, 512), (1, 512, 256), (1, 768, 256))
AHEAD = 3
VLIM = 56
CUTS = 8
GPIECES = ((0, 0, 512), (0, 512, 512), (1, 0, 512), (1, 512, 512))


def mm(a, b):
    return jnp.dot(a, b, preferred_element_type=f32)


def cols(i, width):
    return pl.ds(pl.multiple_of(i * width, width), width)


def nt(a, b):
    return lax.dot_general(a, b, (((1,), (1,)), ((), ())), preferred_element_type=f32)


def tn(a, b):
    return lax.dot_general(a, b, (((0,), (0,)), ((), ())), preferred_element_type=f32)


def kernel(
    scale,
    lat, ei, ew, truth, w, wot,
    gl, gh, go,
    xw, at, a, wv, wotr, wotv, eiv, ewv, trr, trv,
    agg, pre, act, fcs, fcr, dfs, dfr, dpre, daggc,
    low, up, rlow, rup, own,
    ghk, ghs, ghr, ys, yr, xk, xs, xr, zs, zr, ghv,
    gok, gos, gor, gzk, gzs, gzr, gxs, gxr, gyv, gyr,
    ld, fs, fr, es, er, bs, br, hs, hr, cs, cr, ysm, yrm, xsm, xrm, zsm, zrm, gsm, grm,
    gzsm, gzrm, gxsm, gxrm, gysm, gyrm, outsm,
):
    e = lax.axis_index("ens")
    s = lax.axis_index("space")
    z = s // 8
    x = (s // 2) % NX
    core = s % 2
    right = (e, (s + 1) % SPACE)
    left = (e, (s + SPACE - 1) % SPACE)
    mate = (e, z * 8 + x * 2 + (1 - core))
    ypeer = [((e + k) % ENS, s) for k in range(1, ENS)]
    xpeer = [(e, z * 8 + ((x + k) % NX) * 2 + core) for k in range(1, NX)]
    zpeer = [(e, ((z + k) % NZ) * 8 + x * 2 + core) for k in range(1, NZ)]

    def remote(src, dst, ssem, rsem, to):
        cp = pltpu.make_async_remote_copy(
            src_ref=src, dst_ref=dst, send_sem=ssem, recv_sem=rsem, device_id=to, device_id_type=MESH
        )
        sends.append(cp)
        return cp

    sends = []
    barrier = pltpu.get_barrier_semaphore()
    everyone = [left, right, mate] + ypeer + xpeer + zpeer
    for to in everyone:
        pl.semaphore_signal(barrier, inc=1, device_id=to, device_id_type=MESH)

    loads = [
        pltpu.make_async_copy(ei, eiv, ld.at[0]),
        pltpu.make_async_copy(ew, ewv, ld.at[1]),
        pltpu.make_async_copy(lat, xw.at[:, pl.ds(NB, NB)], ld.at[2]),
        pltpu.make_async_copy(w, wv, ld.at[3]),
        pltpu.make_async_copy(wot, wotr, ld.at[4]),
        pltpu.make_async_copy(truth.at[:, cols(e, QG)], trr, ld.at[5]),
    ]
    for cp in loads:
        cp.start()
    pl.semaphore_wait(barrier, len(everyone))

    halo = {}

    def send_halo(i):
        m, first, width = PIECES[i]
        part = lat.at[m, :, pl.ds(first, width)]
        up_cp = remote(part, xw.at[m, pl.ds(0, NB), pl.ds(first, width)], fs.at[0, i], fr.at[0, i], right)
        dn_cp = remote(part, xw.at[m, pl.ds(2 * NB, NB), pl.ds(first, width)], fs.at[1, i], fr.at[1, i], left)
        up_cp.start()
        dn_cp.start()
        halo[i] = (up_cp, dn_cp)

    for i in range(AHEAD):
        send_halo(i)

    loads[0].wait()
    loads[1].wait()
    wr = ewv[...].astype(bf16).astype(f32)

    @pl.loop(0, 3 * NB // 128)
    def _(b):
        row = lax.broadcasted_iota(jnp.int32, (128, G), 0) + b * 128
        t = jnp.zeros((128, G), f32)
        for k in range(4):
            t = jnp.where(row == eiv[pl.ds(k, 1), :], wr[k : k + 1, :], t)
        at[cols(b, 128), :] = t.astype(bf16)
        a[:, cols(b, 128)] = t.T.astype(bf16)

    for cp in loads[2:]:
        cp.wait()
    wotv[...] = jnp.concatenate([wotr[...], jnp.zeros((VP - V, H), bf16)], axis=0)
    trv[...] = jnp.concatenate([trr[...], jnp.zeros((VM - V, QG), f32)], axis=0)
    for k in range(ENS):
        for m in range(2):
            fcr[k, m, pl.ds(VS, VM - VS), :] = jnp.zeros((VM - VS, QG), f32)
    for m in range(2):
        dfr[m, pl.ds(VM, VP - VM), :] = jnp.zeros((VP - VM, G), bf16)

    def slope(m):
        @pl.loop(0, H // 256)
        def _(t):
            v = pre[m, :, cols(t, 256)]
            sg = jax.nn.sigmoid(v)
            pre[m, :, cols(t, 256)] = sg * (1.0 + v * (1.0 - sg))

    for i, (m, first, width) in enumerate(PIECES):
        for cp in halo[i]:
            cp.wait_recv()
        if i + AHEAD < len(PIECES):
            send_halo(i + AHEAD)
        part = pl.ds(first, width)
        agg[pl.ds(m * G, G), part] = mm(a[...], xw[m, :, part]).astype(bf16)
        v = mm(agg[pl.ds(m * G, G), part], wv[part, :])
        if first > 0:
            v = v + pre[m]
        pre[m] = v
        if first + width < H:
            continue
        for k in range(ENS):
            r = (e + 1 + k) % ENS
            rows = cols(r, QG)
            arows = pl.ds(pl.multiple_of(m * G + r * QG, QG), QG)
            v = pre[m, rows, :]
            act[arows, :] = (v * jax.nn.sigmoid(v)).astype(bf16)
            fc = nt(wotv[pl.ds(0, VM), :], act[arows, :])
            if k < ENS - 1:
                fcs[k, m] = fc[:VS]
                remote(
                    fcs.at[k, m], fcr.at[k, m, pl.ds(0, VS)], es.at[k, m], er.at[k, m], ypeer[k]
                ).start()
            else:
                fcr[k, m, pl.ds(0, VS), :] = fc[:VS]
        slope(m)

    for m in range(2):
        for k in range(ENS - 1):
            pltpu.make_async_remote_copy(
                src_ref=fcs.at[k, m], dst_ref=fcr.at[k, m, pl.ds(0, VS)], send_sem=es.at[k, m],
                recv_sem=er.at[k, m], device_id=ypeer[k], device_id_type=MESH,
            ).wait_recv()

    members = 2 * ENS

    @pl.loop(0, VM // 16)
    def _(b):
        rows = cols(b, 16)
        f = [fcr[i // 2, i % 2, rows, :] for i in range(members)]
        tr = trv[rows, :]
        total = [jnp.zeros((16, QG), f32) for _ in range(members)]
        for i in range(members):
            for j in range(i + 1, members):
                d = f[i] - f[j]
                q = d * lax.rsqrt(d * d + smoothing * smoothing)
                total[i] = total[i] + q
                total[j] = total[j] - q
        for i in range(members):
            d = f[i] - tr
            q = d * lax.rsqrt(d * d + smoothing * smoothing)
            dfs[i // 2, i % 2, rows, :] = (
                scale * (q * (1.0 / members) - total[i] * (1.0 / (members * (members - 1))))
            ).astype(bf16)

    for m in range(2):
        for k in range(ENS - 1):
            back = ((e + ENS - 1 - k) % ENS, s)
            remote(
                dfs.at[k, m], dfr.at[m, pl.ds(0, VM), cols(e, QG)], bs.at[k, m], br.at[k, m], back
            ).start()
        dfr[m, pl.ds(0, VM), cols(e, QG)] = dfs[ENS - 1, m]

    def dpreact(m):
        for k in range(ENS - 1):
            src = (e + 1 + k) % ENS
            pltpu.make_async_remote_copy(
                src_ref=dfs.at[k, m], dst_ref=dfr.at[m, pl.ds(0, VM), cols(src, QG)], send_sem=bs.at[k, m],
                recv_sem=br.at[k, m], device_id=((e + ENS - 1 - k) % ENS, s), device_id_type=MESH,
            ).wait_recv()
        dpre[pl.ds(m * G, G), :] = (tn(dfr[m], wotv[...]) * pre[m]).astype(bf16)

    RJ = H // NJ
    NG = RJ // 32
    gcore = []
    ycp = []

    def send_y(j):
        gcore[j].wait_recv()
        groups = pl.ds(j * NG, NG)
        v = ghk[groups] + ghr[groups].astype(f32)
        ghk[groups] = v
        for k in range(ENS):
            ys[k, groups] = v[:, :, k * QC : (k + 1) * QC].astype(bf16)
        for k in range(1, ENS):
            cp = remote(
                ys.at[(e + k) % ENS, groups], yr.at[k - 1, groups], ysm.at[k - 1, j],
                yrm.at[k - 1, j], ypeer[k - 1],
            )
            cp.start()
            ycp.append(cp)

    grads = []

    def node_grads(i):
        m, first, width = GPIECES[i]
        part = pl.ds(first, width)
        daggc[:, pl.ds(0, width)] = nt(dpre[pl.ds(m * G, G), :], wv[part, :]).astype(bf16)
        v = mm(at[...], daggc[:, pl.ds(0, width)])
        low[i] = v[:NB].astype(bf16)
        up[i] = v[2 * NB :].astype(bf16)
        own[m, :, part] = v[NB : 2 * NB]
        one = remote(low.at[i], rlow.at[i], hs.at[0, i], hr.at[0, i], left)
        two = remote(up.at[i], rup.at[i], hs.at[1, i], hr.at[1, i], right)
        one.start()
        two.start()
        grads.append((one, two))

    dpreact(0)
    node_grads(0)
    node_grads(1)
    dpreact(1)
    for j in range(NJ):
        v = tn(agg[:, pl.ds(j * RJ, RJ)], dpre[...]).reshape(NG, 2, 16, H)
        groups = pl.ds(j * NG, NG)
        ghk[groups] = jnp.where(core == 0, v[:, 0], v[:, 1])
        ghs[groups] = jnp.where(core == 0, v[:, 1], v[:, 0]).astype(bf16)
        cp = remote(ghs.at[groups], ghr.at[groups], cs.at[j], cr.at[j], mate)
        cp.start()
        gcore.append(cp)
        if j >= LAG:
            send_y(j - LAG)
    node_grads(2)
    for j in range(NJ - LAG, NJ):
        send_y(j)
    for i in range(3, len(GPIECES)):
        node_grads(i)

    v = mm(dfr[0], act[pl.ds(0, G), :]) + mm(dfr[1], act[pl.ds(G, G), :])
    v = v.T.reshape(H // 32, 2, 16, VP)
    gok[...] = jnp.where(core == 0, v[:, 0], v[:, 1])
    gos[...] = jnp.where(core == 0, v[:, 1], v[:, 0]).astype(bf16)
    gcp = remote(gos, gor, gsm.at[0], grm.at[0], mate)
    gcp.start()
    gcp.wait_recv()
    gzs[...] = (gok[...] + gor[...].astype(f32)).astype(bf16)
    gz = []
    for k in range(1, NZ):
        cp = remote(gzs.at[cols((z + k) % NZ, NX)], gzr.at[k - 1], gzsm.at[k - 1], gzrm.at[k - 1], zpeer[k - 1])
        cp.start()
        gz.append(cp)
    gzk[...] = gok[cols(z, NX)] + gor[cols(z, NX)].astype(f32)

    for cp in gz:
        cp.wait_recv()
    v = gzk[...]
    for k in range(NZ - 1):
        v = v + gzr[k].astype(f32)
    gzk[...] = v
    gxs[...] = v.astype(bf16)
    gx = []
    for k in range(1, NX):
        cp = remote(gxs.at[(x + k) % NX], gxr.at[k - 1], gxsm.at[k - 1], gxrm.at[k - 1], xpeer[k - 1])
        cp.start()
        gx.append(cp)

    xcp = []

    def send_x(j):
        for k in range(ENS - 1):
            ycp[j * (ENS - 1) + k].wait_recv()
        groups = pl.ds(j * NG, NG)
        v = ghk[groups, :, cols(e, QC)]
        for k in range(ENS - 1):
            v = v + yr[k, groups].astype(f32)
        zz = pl.ds(j * ZJ, ZJ)
        xk[zz] = v.reshape(ZJ, NX, 16, QC)
        for k in range(NX):
            xs[k, zz] = xk[zz, k].astype(bf16)
        for k in range(1, NX):
            cp = remote(
                xs.at[(x + k) % NX, zz], xr.at[k - 1, zz], xsm.at[k - 1, j], xrm.at[k - 1, j], xpeer[k - 1]
            )
            cp.start()
            xcp.append(cp)

    def add_x(j):
        for k in range(NX - 1):
            xcp[j * (NX - 1) + k].wait_recv()
        zz = pl.ds(j * ZJ, ZJ)
        v = xk[zz, x]
        for k in range(NX - 1):
            v = v + xr[k, zz].astype(f32)
        xk[zz, x] = v
        zs[zz] = v.astype(bf16)

    outs = []

    def finish(i):
        m, first, width = GPIECES[i]
        for cp in grads[i]:
            cp.wait_recv()
        part = pl.ds(first, width)
        own[m, :, part] = own[m, :, part] + rlow[i].astype(f32) + rup[i].astype(f32)
        cp = pltpu.make_async_copy(own.at[m, :, part], gl.at[m, :, part], outsm.at[i])
        cp.start()
        outs.append(cp)

    left_over = list(range(len(GPIECES)))
    for j in range(NJ):
        send_x(j)
        if j >= 1:
            add_x(j - 1)
        if j < NJ - 1:
            finish(left_over.pop(0))

    for cp in gx:
        cp.wait_recv()
    v = gzk[x]
    for k in range(NX - 1):
        v = v + gxr[k].astype(f32)
    gyv[...] = v
    gy = []
    for k in range(1, ENS):
        cp = remote(gyv, gyr.at[k - 1], gysm.at[k - 1], gyrm.at[k - 1], ypeer[k - 1])
        cp.start()
        gy.append(cp)

    add_x(NJ - 1)
    zcp = []
    for k in range(1, NZ):
        cp = remote(zs.at[(z + k) % NZ], zr.at[k - 1], zsm.at[k - 1], zrm.at[k - 1], zpeer[k - 1])
        cp.start()
        zcp.append(cp)
    for i in left_over:
        finish(i)
    for cp in gy:
        cp.wait_recv()
    v = gyv[...]
    for k in range(ENS - 1):
        v = v + gyr[k]
    go[...] = v[:, :V]
    for cp in zcp:
        cp.wait_recv()
    v = xk[z, x]
    for k in range(NZ - 1):
        v = v + zr[k].astype(f32)
    ghv[:, cols(e, QC)] = v
    for k in range(1, ENS):
        mine = ghv.at[:, cols(e, QC)]
        remote(mine, mine, gsm.at[k], grm.at[k], ypeer[k - 1]).start()
    for k in range(1, ENS):
        src = (e + ENS - k) % ENS
        theirs = ghv.at[:, cols(src, QC)]
        pltpu.make_async_remote_copy(
            src_ref=theirs, dst_ref=theirs, send_sem=gsm.at[k], recv_sem=grm.at[k],
            device_id=ypeer[k - 1], device_id_type=MESH,
        ).wait_recv()
    gh[...] = ghv[...]
    for cp in outs:
        cp.wait()
    for cp in sends:
        cp.wait_send()


def hand_over(a, b, c, oa, ob, oc, va, vb, vc, isem, osem):
    rows = a.shape[1] // CUTS * 2
    places = [(i % 2, pl.ds(i // 2 * rows, rows)) for i in range(CUTS)]
    moves = [(a.at[p], va.at[p], oa.at[p]) for p in places] + [(b, vb, ob), (c, vc, oc)]
    ins = [pltpu.make_async_copy(src, mid, isem.at[i]) for i, (src, mid, _) in enumerate(moves)]
    outs = [pltpu.make_async_copy(mid, dst, osem.at[i]) for i, (_, mid, dst) in enumerate(moves)]
    for cp in ins:
        cp.start()
    for one, two in zip(ins, outs):
        one.wait()
        two.start()
    for cp in outs:
        cp.wait()


def shards(latents, edge_index, edge_weight, truth, w_hidden, output_weight):
    members = latents.shape[0] * lax.axis_size("ens")
    cells = truth.shape[1] * lax.axis_size("space")
    scale = 1.0 / math.sqrt(cells * members)
    any_ = pl.BlockSpec(memory_space=pl.ANY)
    vm = pl.BlockSpec(memory_space=pltpu.VMEM)
    dma = pltpu.SemaphoreType.DMA
    R2 = H // 32
    scratch = [
        pltpu.VMEM((2, 3 * NB, H), bf16),
        pltpu.VMEM((3 * NB, G), bf16),
        pltpu.VMEM((G, 3 * NB), bf16),
        pltpu.VMEM((H, H), bf16),
        pltpu.VMEM((V, H), bf16),
        pltpu.VMEM((VP, H), bf16),
        pltpu.VMEM((4, G), jnp.int32),
        pltpu.VMEM((4, G), f32),
        pltpu.VMEM((V, QG), f32),
        pltpu.VMEM((VM, QG), f32),
        pltpu.VMEM((2 * G, H), bf16),
        pltpu.VMEM((2, G, H), f32),
        pltpu.VMEM((2 * G, H), bf16),
        pltpu.VMEM((ENS - 1, 2, VS, QG), f32),
        pltpu.VMEM((ENS, 2, VM, QG), f32),
        pltpu.VMEM((ENS, 2, VM, QG), bf16),
        pltpu.VMEM((2, VP, G), bf16),
        pltpu.VMEM((2 * G, H), bf16),
        pltpu.VMEM((G, 512), bf16),
        pltpu.VMEM((len(GPIECES), NB, 512), bf16),
        pltpu.VMEM((len(GPIECES), NB, 512), bf16),
        pltpu.VMEM((len(GPIECES), NB, 512), bf16),
        pltpu.VMEM((len(GPIECES), NB, 512), bf16),
        pltpu.VMEM((2, NB, H), f32),
        pltpu.VMEM((R2, 16, H), f32),
        pltpu.VMEM((R2, 16, H), bf16),
        pltpu.VMEM((R2, 16, H), bf16),
        pltpu.VMEM((ENS, R2, 16, QC), bf16),
        pltpu.VMEM((ENS - 1, R2, 16, QC), bf16),
        pltpu.VMEM((NZ, NX, 16, QC), f32),
        pltpu.VMEM((NX, NZ, 16, QC), bf16),
        pltpu.VMEM((NX - 1, NZ, 16, QC), bf16),
        pltpu.VMEM((NZ, 16, QC), bf16),
        pltpu.VMEM((NZ - 1, 16, QC), bf16),
        pltpu.VMEM((16, H), f32),
        pltpu.VMEM((R2, 16, VP), f32),
        pltpu.VMEM((R2, 16, VP), bf16),
        pltpu.VMEM((R2, 16, VP), bf16),
        pltpu.VMEM((NX, 16, VP), f32),
        pltpu.VMEM((R2, 16, VP), bf16),
        pltpu.VMEM((NZ - 1, NX, 16, VP), bf16),
        pltpu.VMEM((NX, 16, VP), bf16),
        pltpu.VMEM((NX - 1, 16, VP), bf16),
        pltpu.VMEM((16, VP), f32),
        pltpu.VMEM((ENS - 1, 16, VP), f32),
        dma((6,)),
        dma((2, len(PIECES))), dma((2, len(PIECES))),
        dma((ENS - 1, 2)), dma((ENS - 1, 2)),
        dma((ENS - 1, 2)), dma((ENS - 1, 2)),
        dma((2, len(GPIECES))), dma((2, len(GPIECES))),
        dma((NJ,)), dma((NJ,)),
        dma((ENS - 1, NJ)), dma((ENS - 1, NJ)),
        dma((NX - 1, NJ)), dma((NX - 1, NJ)),
        dma((NZ - 1,)), dma((NZ - 1,)),
        dma((ENS,)), dma((ENS,)),
        dma((NZ - 1,)), dma((NZ - 1,)),
        dma((NX - 1,)), dma((NX - 1,)),
        dma((ENS - 1,)), dma((ENS - 1,)),
        dma((len(GPIECES),)),
    ]
    held = pl.pallas_call(
        functools.partial(kernel, scale),
        out_shape=(
            jax.ShapeDtypeStruct((2, NB, H), f32),
            jax.ShapeDtypeStruct((16, H), f32),
            jax.ShapeDtypeStruct((16, V), f32),
        ),
        in_specs=[any_] * 6,
        out_specs=(any_, vm, vm),
        scratch_shapes=scratch,
        compiler_params=pltpu.CompilerParams(
            collective_id=0, has_side_effects=True, vmem_limit_bytes=VLIM << 20
        ),
        name="decoder",
    )(latents, edge_index.T, edge_weight.T, truth, w_hidden, output_weight.T)
    return pl.pallas_call(
        hand_over,
        out_shape=[jax.ShapeDtypeStruct(v.shape, v.dtype) for v in held],
        in_specs=[any_] * 3,
        out_specs=[any_] * 3,
        scratch_shapes=[pltpu.VMEM(v.shape, v.dtype) for v in held] + [dma((CUTS + 2,)), dma((CUTS + 2,))],
        name="hand_over",
    )(*held)


def solution(mesh):
    placed = (
        P("ens", "space", None),
        P("space", None),
        P("space", None),
        P(None, "space"),
        P(),
        P(),
    )
    return jax.shard_map(
        shards,
        mesh=mesh,
        in_specs=placed,
        out_specs=(P("ens", "space", None), P("space", None), P("space", None)),
        check_vma=False,
    )
```
